32 devices in a mesh: dom: 16 (over z, y, core), sub: 2 (over x).
Axes of the slice: x: 2, y: 2, z: 4, core: 2. Of those that a mesh axis runs over, the one named last changes fastest.
Arguments:
- modal_state: float32 [35, 9, 4096], P(None, None, ('dom', 'sub')), may hold values from -6 to 6
- star_matrices: float32 [3, 9, 9, 4096], P(None, None, None, ('dom', 'sub')), may hold values from -2 to 2
- face_normals: float32 [3, 4, 4096], P(None, None, ('dom', 'sub')), may hold values from -4 to 4
- wave_speed: float32 [4096], P(('dom', 'sub')), may hold values from 1 to 3
- inverse_jacobian: float32 [4096], P(('dom', 'sub')), may hold values from 0.02 to 0.2
- stiffness: float32 [3, 35, 35], replicated, may hold values from -1 to 1
- lift_minus: float32 [4, 35, 35], replicated, may hold values from -1 to 1
- lift_plus: float32 [4, 35, 35], replicated, may hold values from -1 to 1
- cluster: int32 [4096], P(('dom', 'sub')), may hold values from 0 to 1, as said below
- face_source: int32 [4, 4096], P(None, ('dom', 'sub')), may hold values from 0 to 167, as said below
- send_rows: int32 [32, 2, 5, 2, 4], P(('dom', 'sub')), may hold values from 0 to 127
- send_counts: int32 [32, 2, 5, 2], P(('dom', 'sub')), may hold values from 0 to 4, as said below
Outputs:
- new_state: float32 [35, 9, 4096], P(None, None, ('dom', 'sub'))
The draws below stay inside these ranges and needn't reach their ends.
Inputs may be any that keep to these rules, and one draw needn't show every extreme that they name: At most 16 elements of one device have cluster 0, and some device has exactly 16. `face_source`: values below 128 name a local element; a larger value names a row of the receive pool of the element's own cluster list. `send_counts`: zero for a device's own slot (offset 2, its own sub index) and for targets beyond the ends of dom; some count equals 4.
All inputs are finite; a program needn't handle non-finite values.
Results may differ from the reference program's by a relative error of at most 0.0003.
Values sent between devices are 32-bit elements; how exact they have to be, the bound alone decides.
A program may use at most 64 MiB of HBM per device.

```python
import math
import jax
import jax.numpy as jnp
from jax import lax

BASIS = 35
QUANTS = 9
DEGREE = 4
SPAN = 2
ELEM_DEV = 128
FINE_CAP = 16
SLOT_CAP = 4
ELEMENTS = 4096
OFFSETS = 5
POOL = 40
N_DOM = 16
N_SUB = 2


def draw_cluster(key, part):
    count_key, choose_key, order_key = jax.random.split(key, 3)
    device_total = N_DOM * N_SUB
    base_draw = jax.random.randint(count_key, (device_total,), 1, FINE_CAP + 1)
    fine_counts = base_draw * base_draw // FINE_CAP
    chosen = jax.random.randint(choose_key, (), 0, device_total)
    fine_counts = jnp.where(jnp.arange(device_total) == chosen, FINE_CAP, fine_counts)
    ordering = jax.vmap(lambda sub_key: jax.random.permutation(sub_key, ELEM_DEV))(jax.random.split(order_key, device_total))
    is_fine = ordering < fine_counts[:, None]
    return jnp.where(is_fine, 0, 1).astype(jnp.int32).reshape(-1)


def draw_face_source(key, part):
    kind_key, local_key, remote_key = jax.random.split(key, 3)
    layout = (4, ELEMENTS)
    remote = jax.random.randint(kind_key, layout, 0, 8) < 3
    local_rows = jax.random.randint(local_key, layout, 0, ELEM_DEV)
    pool_rows = ELEM_DEV + jax.random.randint(remote_key, layout, 0, POOL)
    picked = jnp.where(remote, pool_rows, local_rows)
    picked = picked.at[0, 0].set(ELEM_DEV + POOL - 1).at[1, 0].set(0)
    return picked.astype(jnp.int32)


def draw_send_counts(key, part):
    amount_key, link_key = jax.random.split(key)
    layout = (N_DOM * N_SUB, 2, 2 * SPAN + 1, N_SUB)
    amounts = jax.random.randint(amount_key, layout, SLOT_CAP // 2, SLOT_CAP + 1)
    linked = jax.random.randint(link_key, layout, 0, 4) > 0
    device = lax.broadcasted_iota(jnp.int32, layout, 0)
    offset = lax.broadcasted_iota(jnp.int32, layout, 2) - SPAN
    target = lax.broadcasted_iota(jnp.int32, layout, 3)
    dom_target = device // N_SUB + offset
    allowed = (dom_target >= 0) & (dom_target < N_DOM) & ((offset != 0) | (target != device % N_SUB))
    amounts = jnp.where(linked & allowed, amounts, 0)
    amounts = amounts.at[0, 0, SPAN + 1, 0].set(SLOT_CAP)
    return amounts.astype(jnp.int32)


def with_ends(values, rng, least, top_value):
    dims = values.shape
    spot = [jax.random.randint(jax.random.fold_in(rng, axis), (), 0, dims[axis]) for axis in range(len(dims))]
    values = values.at[tuple(spot)].set(least)
    longest = dims.index(max(dims))
    spot[longest] = (spot[longest] + 1) % dims[longest]
    return values.at[tuple(spot)].set(top_value)


def block_levels(own_key, dims, cuts, least, top_value):
    loudness, own = 1.0, jax.random.fold_in(own_key, 6)
    for position, parts in cuts:
        draws = jnp.exp(jax.random.uniform(jax.random.fold_in(own, position), (parts,), jnp.float32, least / len(cuts), top_value / len(cuts)))
        loudness = loudness * jnp.repeat(draws, dims[position] // parts).reshape([-1 if axis == position else 1 for axis in range(len(dims))])
    return loudness


def centred(rng, shape, width, bound, pieces=(), kind=jnp.bfloat16):
    result = jax.random.normal(rng, shape, jnp.float32) * width
    if len(pieces) > 0:
        result = block_levels(rng, shape, pieces, -0.22, 0.18) * result
    return jnp.clip(result, min=-bound, max=bound).astype(kind)


def setup_inputs(seed: int = 0) -> dict:
    seeds = jax.random.split(jax.random.key(seed), 13)
    modal_state = centred(seeds[0], (BASIS, QUANTS, ELEMENTS), 1.0, 6.0, ((2, 32),), jnp.float32)
    star_matrices = centred(seeds[1], (3, QUANTS, QUANTS, ELEMENTS), QUANTS ** -0.5, 2.0, ((3, 32),), jnp.float32)
    face_normals = centred(seeds[2], (3, 4, ELEMENTS), 1.0, 4.0, ((2, 32),), jnp.float32)
    wave_speed = jnp.clip(jnp.exp(math.log(3.0) - 1.0986123 * jax.random.uniform(seeds[3], (ELEMENTS,), jnp.float32) ** block_levels(seeds[3], (ELEMENTS,), ((0, 32),), -0.2, 0.2)), 1.0, 3.0)
    inverse_jacobian = jnp.clip(jnp.exp(math.log(0.2) - 2.3025851 * jax.random.uniform(seeds[4], (ELEMENTS,), jnp.float32) ** block_levels(seeds[4], (ELEMENTS,), ((0, 32),), -0.2, 0.2)), 0.02, 0.2)
    stiffness = centred(seeds[5], (3, BASIS, BASIS), BASIS ** -0.5, 1.0, (), jnp.float32)
    lift_minus = centred(seeds[6], (4, BASIS, BASIS), BASIS ** -0.5, 1.0, (), jnp.float32)
    lift_plus = centred(seeds[7], (4, BASIS, BASIS), BASIS ** -0.5, 1.0, (), jnp.float32)
    cluster = draw_cluster(jax.random.fold_in(seeds[12], 71), 0)
    face_source = draw_face_source(jax.random.fold_in(seeds[12], 71), 0)
    send_rows = with_ends(jax.random.randint(seeds[10], (N_DOM * N_SUB, 2, OFFSETS, N_SUB, SLOT_CAP), 0, ELEM_DEV), jax.random.fold_in(seeds[10], 1), 0, ELEM_DEV - 1).astype(jnp.int32)
    send_counts = draw_send_counts(jax.random.fold_in(seeds[12], 71), 0)
    return {"modal_state": modal_state, "star_matrices": star_matrices, "face_normals": face_normals, "wave_speed": wave_speed, "inverse_jacobian": inverse_jacobian, "stiffness": stiffness, "lift_minus": lift_minus, "lift_plus": lift_plus, "cluster": cluster, "face_source": face_source, "send_rows": send_rows, "send_counts": send_counts}


half_step = 0.5
top_precision = lax.Precision.HIGHEST


def quantity_mix(values, matrices):
    total = values[:, 0:1, :] * matrices[0][None]
    for inner in range(1, values.shape[1]):
        total = total + values[:, inner:inner + 1, :] * matrices[inner][None]
    return total


def basis_mix(matrix, values):
    return jnp.einsum("cb,bqe->cqe", matrix, values, precision=top_precision)


def basis_mix_back(matrix, values):
    return jnp.einsum("bc,bqe->cqe", matrix, values, precision=top_precision)


def derivative(values, star_local, stiffness):
    summed = basis_mix(stiffness[0], quantity_mix(values, star_local[0]))
    for direction in range(1, 3):
        summed = summed + basis_mix(stiffness[direction], quantity_mix(values, star_local[direction]))
    return -summed


def integrals(values, star_local, stiffness, intervals):
    results = [(upper_time - lower_time) * values for lower_time, upper_time in intervals]
    current = values
    for degree_now in range(1, DEGREE + 1):
        current = derivative(current, star_local, stiffness)
        factor = float(math.factorial(degree_now + 1))
        results = [acc_value + ((upper_time ** (degree_now + 1) - lower_time ** (degree_now + 1)) / factor) * current for acc_value, (lower_time, upper_time) in zip(results, intervals)]
    return results


def update(integral, sources, star_local, normal_local, speed_local, stiffness, lift_minus, lift_plus):
    summed = basis_mix_back(stiffness[0], quantity_mix(integral, star_local[0]))
    for direction in range(1, 3):
        summed = summed + basis_mix_back(stiffness[direction], quantity_mix(integral, star_local[direction]))
    for face_index in range(4):
        normal_mats = normal_local[0, face_index][None, None, :] * star_local[0]
        for direction in range(1, 3):
            normal_mats = normal_mats + normal_local[direction, face_index][None, None, :] * star_local[direction]
        inner_flux = 0.5 * quantity_mix(integral, normal_mats) + 0.5 * speed_local * integral
        outer_flux = 0.5 * quantity_mix(sources[face_index], normal_mats) - 0.5 * speed_local * sources[face_index]
        summed = summed - basis_mix(lift_minus[face_index], inner_flux) - basis_mix(lift_plus[face_index], outer_flux)
    return summed


def neighbours(local_values, pool_rows, face_rows):
    joined = jnp.concatenate([local_values, pool_rows], axis=2)
    return [jnp.take(joined, face_rows[face_index], axis=2) for face_index in range(4)]


def outgoing(values, slot_rows, slot_counts):
    picked = jnp.take(values, slot_rows.reshape(-1), axis=2)
    picked = picked.reshape((values.shape[0], values.shape[1]) + slot_rows.shape)
    live_slots = lax.broadcasted_iota(jnp.int32, slot_rows.shape, 2) < slot_counts[:, :, None]
    return jnp.where(live_slots[None, None], picked, jnp.zeros_like(picked))


def pull(blocks, device):
    dom_index = device // N_SUB
    sub_index = device % N_SUB
    offset_ids = jnp.arange(2 * SPAN + 1, dtype=jnp.int32)
    source_dom = dom_index - (offset_ids - SPAN)
    valid_source = (source_dom >= 0) & (source_dom < N_DOM)
    source = jnp.clip(source_dom, 0, N_DOM - 1)[:, None] * N_SUB + jnp.arange(N_SUB, dtype=jnp.int32)[None, :]
    taken_rows = blocks[source, :, :, offset_ids[:, None], sub_index, :]
    taken_rows = jnp.where(valid_source[:, None, None, None, None], taken_rows, jnp.zeros_like(taken_rows))
    return jnp.transpose(taken_rows, (2, 3, 0, 1, 4)).reshape(BASIS, QUANTS, POOL)


def reference(modal_state, star_matrices, face_normals, wave_speed, inverse_jacobian, stiffness, lift_minus, lift_plus, cluster, face_source, send_rows, send_counts):
    devices_all = jnp.arange(N_DOM * N_SUB, dtype=jnp.int32)
    intervals = ((0.0, half_step), (half_step, 2.0 * half_step))

    def local(operand, device):
        return lax.dynamic_slice_in_dim(operand, device * ELEM_DEV, ELEM_DEV, operand.ndim - 1)

    def opening(device):
        state_now = local(modal_state, device)
        star_local = local(star_matrices, device)
        early_int, late_int = integrals(state_now, star_local, stiffness, intervals)
        return state_now, star_local, early_int, late_int

    def section_one(device):
        early_int = opening(device)[2]
        return outgoing(early_int, send_rows[device, 0], send_counts[device, 0])

    first_blocks = lax.map(section_one, devices_all)

    def middle(device):
        state_now, star_local, early_int, late_int = opening(device)
        normal_local = local(face_normals, device)
        speed_local = local(wave_speed, device)
        jacobian_local = local(inverse_jacobian, device)
        faces_local = local(face_source, device)
        is_fine = local(cluster, device) == 0
        first_pool = pull(first_blocks, device)
        sources = neighbours(early_int, first_pool, faces_local)
        fine_mid = state_now + jacobian_local * update(early_int, sources, star_local, normal_local, speed_local, stiffness, lift_minus, lift_plus)
        fine_int = integrals(fine_mid, star_local, stiffness, ((0.0, half_step),))[0]
        fine_value = jnp.where(is_fine, fine_int, late_int)
        coarse_value = early_int + fine_value
        return state_now, star_local, normal_local, speed_local, jacobian_local, faces_local, is_fine, fine_mid, fine_int, fine_value, coarse_value

    def section_two(device):
        parts_now = middle(device)
        fine_value, coarse_value = parts_now[9], parts_now[10]
        return (outgoing(fine_value, send_rows[device, 0], send_counts[device, 0]), outgoing(coarse_value, send_rows[device, 1], send_counts[device, 1]))

    second_blocks, coarse_blocks = lax.map(section_two, devices_all)

    def section_three(device):
        state_now, star_local, normal_local, speed_local, jacobian_local, faces_local, is_fine, fine_mid, fine_int, fine_value, coarse_value = middle(device)
        second_pool = pull(second_blocks, device)
        coarse_pool = pull(coarse_blocks, device)
        fine_end = fine_mid + jacobian_local * update(fine_int, neighbours(fine_value, second_pool, faces_local), star_local, normal_local, speed_local, stiffness, lift_minus, lift_plus)
        coarse_end = state_now + jacobian_local * update(coarse_value, neighbours(coarse_value, coarse_pool, faces_local), star_local, normal_local, speed_local, stiffness, lift_minus, lift_plus)
        return jnp.where(is_fine, fine_end, coarse_end)

    new_state = lax.map(section_three, devices_all)
    return jnp.transpose(new_state, (1, 2, 0, 3)).reshape(BASIS, QUANTS, ELEMENTS)
```

```python
import functools
import math

import jax
import jax.numpy as jnp
from jax import lax
from jax.experimental import pallas as pl
from jax.experimental.pallas import tpu as pltpu
from jax.sharding import PartitionSpec as P

DEGREE = 4
HALF = 0.5
MESH = pl.DeviceIdType.MESH
f32, bf16 = jnp.float32, jnp.bfloat16


def up(value, step):
    return (value + step - 1) // step * step


def halves(value):
    high = value.astype(bf16).astype(f32)
    return high, value - high


def matmul(left, right, dims=((1,), (0,))):
    return lax.dot_general(
        left.astype(bf16), right.astype(bf16), (dims, ((), ())), preferred_element_type=f32
    )


def pick_coefficient(step, values):
    result = jnp.float32(values[-1])
    for index in range(len(values) - 1):
        result = jnp.where(step == index, jnp.float32(values[index]), result)
    return result


def kernel(
    n_dom,
    n_sub,
    modal,
    star,
    normals,
    speed,
    jacobian,
    stiffness,
    lift_minus,
    lift_plus,
    cluster,
    face_source,
    send_rows,
    send_counts,
    out,
    grad_mat,
    back_mat,
    lift_mat,
    cur,
    early,
    late,
    mid,
    value,
    coarse,
    zed,
    dee,
    faces,
    slot_rows,
    near_hot,
    far_hot,
    send_buf,
    recv_buf,
    send_sem,
    recv_sem,
):
    quants, basis, elems = modal.shape
    rows = cur.shape[0]
    offsets = send_counts.shape[3]
    slots = send_rows.shape[3]
    span = (offsets - 1) // 2
    blocks = offsets * n_sub
    pool_rows = blocks * 2 * slots
    my_dom, my_sub = lax.axis_index("dom"), lax.axis_index("sub")

    def lane(q):
        return slice(q * elems, (q + 1) * elems)

    def partners(step_sign, action):
        for o in range(offsets):
            other = my_dom + step_sign * (o - span)
            for t in range(n_sub):
                good = (other >= 0) & (other < n_dom)
                if o == span:
                    good = my_sub != t

                @pl.when(good)
                def _():
                    action(o, t, other)

    barrier = pltpu.get_barrier_semaphore()
    recv_buf[...] = jnp.zeros_like(recv_buf)

    def greet(o, t, other):
        pl.semaphore_signal(barrier, inc=1, device_id=(other, t), device_id_type=MESH)

    partners(1, greet)

    for scratch in (grad_mat, back_mat, lift_mat, cur):
        scratch[...] = jnp.zeros_like(scratch)

    def place(ref, row, column, matrix):
        high, low = halves(matrix)
        for index, part in enumerate((high, low, high)):
            start = column + index * rows
            ref[row : row + basis, start : start + basis] = part

    for d in range(3):
        place(grad_mat, d * rows, 0, -stiffness[d])
        place(back_mat, d * rows, 0, stiffness[d].T)
    for f in range(4):
        own, far = 0.5 * lift_minus[:, f, :], 0.5 * lift_plus[:, f, :]
        place(lift_mat.at[f], 0, 0, own)
        place(lift_mat.at[f], 0, 3 * rows, far)
        place(lift_mat.at[f], rows, 0, own)
        place(lift_mat.at[f], rows, 3 * rows, -far)

    for q in range(quants):
        cur[:basis, lane(q)] = modal[q]

    coarse_row = cluster[...]
    is_fine = coarse_row == 0
    near_iota = lax.broadcasted_iota(jnp.int32, (elems, elems), 0)
    far_iota = lax.broadcasted_iota(jnp.int32, (pool_rows, elems), 0)
    for f in range(4):
        source = face_source[f : f + 1, :]
        near_hot[:, lane(f)] = jnp.where(near_iota == source, 1.0, 0.0)
        index = source - elems
        block = index // slots
        index = jnp.where(index >= 0, block * (2 * slots) + (index - block * slots) + slots * coarse_row, -1)
        far_hot[:, lane(f)] = jnp.where(far_iota == index, 1.0, 0.0)
    slot_iota = lax.broadcasted_iota(jnp.int32, (slots, elems), 0)
    for o in range(offsets):
        for t in range(n_sub):
            for part in range(2):
                row = ((o * n_sub + t) * 2 + part) * slots
                ids = jnp.broadcast_to(send_rows[0, part, t, :, o : o + 1], (slots, elems))
                live = jnp.broadcast_to(send_counts[0, part, t : t + 1, o : o + 1], (slots, elems))
                slot_rows[row : row + slots, :] = jnp.where(slot_iota < live, ids, -1)
    send_iota = lax.broadcasted_iota(jnp.int32, (pool_rows, elems), 1)
    send_hot = jnp.where(send_iota == slot_rows[...], 1.0, 0.0)
    slot_list = (lax.broadcasted_iota(jnp.int32, (pool_rows, elems), 0) // slots) % 2

    def stacked(source):
        high, low = halves(source)
        return jnp.concatenate([high, high, low], axis=0).astype(bf16)

    def tall(source):
        return jnp.concatenate([source[:, lane(q)] for q in range(quants)], axis=0)

    def mix(finish):
        group = 3
        for first in range(0, quants, group):
            wanted = range(first, min(first + group, quants))
            total = {q: None for q in wanted}
            for d in range(3):
                for p in range(quants):
                    block = zed[d * rows : (d + 1) * rows, lane(p)]
                    for q in wanted:
                        term = block * star[p, q, d : d + 1, :]
                        total[q] = term if total[q] is None else total[q] + term
            for q in wanted:
                finish(q, total[q])

    def expand(sums):
        def step(index, carry):
            zed[...] = matmul(grad_mat[...], stacked(cur[...]))
            scales = [pick_coefficient(index, values) for _, values in sums]

            def finish(q, total):
                cur[:, lane(q)] = total
                for (ref, _), scale in zip(sums, scales):
                    ref[:, lane(q)] = ref[:, lane(q)] + scale * total

            mix(finish)
            return carry

        lax.fori_loop(0, DEGREE, step, 0)

    def weights(low, high):
        return [
            (high ** (k + 1) - low ** (k + 1)) / float(math.factorial(k + 1))
            for k in range(1, DEGREE + 1)
        ]

    def copy(turn, o, t, other):
        block = o * n_sub + my_sub
        return pltpu.make_async_remote_copy(
            src_ref=send_buf.at[turn, o * n_sub + t],
            dst_ref=recv_buf.at[turn, block],
            send_sem=send_sem.at[turn, o * n_sub + t],
            recv_sem=recv_sem.at[turn, block],
            device_id=(other, t),
            device_id_type=MESH,
        )

    def arrival(turn, o, t, other):
        block = o * n_sub + t
        return pltpu.make_async_remote_copy(
            src_ref=send_buf.at[turn, block],
            dst_ref=recv_buf.at[turn, block],
            send_sem=send_sem.at[turn, block],
            recv_sem=recv_sem.at[turn, block],
            device_id=(other, t),
            device_id_type=MESH,
        )

    def send(turn, picked):
        width = picked.shape[1]
        for block in range(blocks):
            first = block * 2 * slots
            send_buf[turn, block, :, :width] = picked[first : first + 2 * slots, :]
        if turn == 0:
            below = jnp.minimum(my_dom, span)
            above = jnp.minimum(n_dom - 1 - my_dom, span)
            pl.semaphore_wait(barrier, (below + above + 1) * n_sub - 1)
        partners(1, lambda o, t, other: copy(turn, o, t, other).start())

    def pick(hot, source):
        high, low = halves(source)
        return matmul(hot, high, ((1,), (1,))) + matmul(hot, low, ((1,), (1,)))

    def update(turn, integral, near_left, near_right, finish):
        high, low = halves(near_left)
        faces[...] = matmul(jnp.concatenate([high, low], axis=0), near_right)
        own = stacked(integral)
        zed[...] = matmul(back_mat[...], own)
        partners(-1, lambda o, t, other: arrival(turn, o, t, other).wait_recv())
        pool = recv_buf[turn].reshape(pool_rows, recv_buf.shape[3])
        high, low = halves(pool.T)
        wide = quants * rows
        faces[...] += matmul(jnp.concatenate([high[:wide], low[:wide]], axis=0), far_hot[...])
        for f in range(4):
            parts = [
                jnp.concatenate(
                    [
                        faces[base + q * rows : base + (q + 1) * rows, lane(f)]
                        for q in range(quants)
                    ],
                    axis=1,
                )
                for base in (0, wide)
            ]
            theirs = jnp.concatenate([parts[0], parts[0], parts[1]], axis=0).astype(bf16)
            lifted = matmul(lift_mat[f, :, : 3 * rows], own) + matmul(
                lift_mat[f, :, 3 * rows :], theirs
            )
            for q in range(quants):
                block = lifted[:rows, lane(q)]
                for d in range(3):
                    zed[d * rows : (d + 1) * rows, lane(q)] -= (
                        normals[d, f : f + 1, :] * block
                    )
                other = lifted[rows:, lane(q)]
                dee[:, lane(q)] = other if f == 0 else dee[:, lane(q)] + other
        mix(lambda q, total: finish(q, total - speed[...] * dee[:, lane(q)]))

    early[...] = HALF * cur[...]
    late[...] = HALF * cur[...]
    mid[...] = cur[...]
    expand([(early, weights(0.0, HALF)), (late, weights(HALF, 2 * HALF))])
    early_tall = tall(early[...])
    send(0, pick(send_hot, early_tall))

    def keep_mid(q, total):
        result = mid[:, lane(q)] + jacobian[...] * total
        cur[:, lane(q)] = result
        value[:, lane(q)] = HALF * result
        mid[:, lane(q)] = jnp.where(is_fine, result, mid[:, lane(q)])

    update(0, early[...], early_tall, near_hot[...], keep_mid)
    expand([(value, weights(0.0, HALF))])
    for q in range(quants):
        fine = jnp.where(is_fine, value[:, lane(q)], late[:, lane(q)])
        value[:, lane(q)] = fine
        coarse[:, lane(q)] = early[:, lane(q)] + fine
    both = jnp.concatenate([tall(value[...]), tall(coarse[...])], axis=1)
    both_hot = jnp.concatenate(
        [jnp.where(slot_list == 0, send_hot, 0.0), jnp.where(slot_list == 1, send_hot, 0.0)], axis=1
    )
    send(1, pick(both_hot, both))
    fine_lanes = jnp.concatenate([is_fine.astype(f32)] * 4, axis=1)
    near_both = jnp.concatenate(
        [near_hot[...] * fine_lanes, near_hot[...] * (1.0 - fine_lanes)], axis=0
    )
    for q in range(quants):
        cur[:, lane(q)] = jnp.where(is_fine, value[:, lane(q)], coarse[:, lane(q)])

    def keep_end(q, total):
        out[q] = (mid[:, lane(q)] + jacobian[...] * total)[:basis]

    update(1, cur[...], both, near_both, keep_end)
    for turn in range(2):
        partners(1, lambda o, t, other: copy(turn, o, t, other).wait_send())


def per_device(n_dom, n_sub, modal_state, star_matrices, face_normals, wave_speed, inverse_jacobian,
               stiffness, lift_minus, lift_plus, cluster, face_source, send_rows, send_counts):
    basis, quants, elems = modal_state.shape
    rows = up(basis, 8)
    wide = quants * elems
    blocks = send_counts.shape[2] * n_sub
    slots = send_rows.shape[4]
    pool_rows = blocks * 2 * slots
    message = (2, blocks, 2 * slots, up(quants * rows, 128))
    state = pltpu.VMEM((rows, wide), f32)
    result = pl.pallas_call(
        functools.partial(kernel, n_dom, n_sub),
        out_shape=jax.ShapeDtypeStruct((quants, basis, elems), f32),
        in_specs=[pl.BlockSpec(memory_space=pltpu.VMEM)] * 12,
        out_specs=pl.BlockSpec(memory_space=pltpu.VMEM),
        scratch_shapes=[
            pltpu.VMEM((3 * rows, 3 * rows), f32),
            pltpu.VMEM((3 * rows, 3 * rows), f32),
            pltpu.VMEM((4, 2 * rows, 6 * rows), f32),
            state,
            state,
            state,
            state,
            state,
            state,
            pltpu.VMEM((3 * rows, wide), f32),
            state,
            pltpu.VMEM((2 * quants * rows, 4 * elems), f32),
            pltpu.VMEM((pool_rows, elems), jnp.int32),
            pltpu.VMEM((elems, 4 * elems), f32),
            pltpu.VMEM((pool_rows, 4 * elems), f32),
            pltpu.VMEM(message, f32),
            pltpu.VMEM(message, f32),
            pltpu.SemaphoreType.DMA((2, blocks)),
            pltpu.SemaphoreType.DMA((2, blocks)),
        ],
        compiler_params=pltpu.CompilerParams(
            collective_id=0, has_side_effects=True, vmem_limit_bytes=32 * 1024 * 1024
        ),
    )(
        modal_state.transpose(1, 0, 2),
        star_matrices.transpose(1, 2, 0, 3),
        face_normals,
        wave_speed[None],
        inverse_jacobian[None],
        stiffness,
        lift_minus.transpose(1, 0, 2),
        lift_plus.transpose(1, 0, 2),
        cluster[None],
        face_source,
        send_rows.transpose(0, 1, 3, 4, 2),
        send_counts.transpose(0, 1, 3, 2),
    )
    return result.transpose(1, 0, 2)


def solution(mesh):
    placed = (
        P(None, None, ("dom", "sub")),
        P(None, None, None, ("dom", "sub")),
        P(None, None, ("dom", "sub")),
        P(("dom", "sub")),
        P(("dom", "sub")),
        P(),
        P(),
        P(),
        P(("dom", "sub")),
        P(None, ("dom", "sub")),
        P(("dom", "sub"), None, None, None, None),
        P(("dom", "sub"), None, None, None),
    )
    return jax.shard_map(
        functools.partial(per_device, mesh.shape["dom"], mesh.shape["sub"]),
        mesh=mesh,
        in_specs=placed,
        out_specs=P(None, None, ("dom", "sub")),
        check_vma=False,
    )
```

```python
import functools
import math

import jax
import jax.numpy as jnp
from jax import lax
from jax.experimental import pallas as pl
from jax.experimental.pallas import tpu as pltpu
from jax.sharding import PartitionSpec as P

DEGREE = 4
HALF = 0.5
MESH = pl.DeviceIdType.MESH
f32, bf16 = jnp.float32, jnp.bfloat16


def up(value, step):
    return (value + step - 1) // step * step


def halves(value):
    high = value.astype(bf16).astype(f32)
    return high, value - high


def matmul(left, right, dims=((1,), (0,))):
    return lax.dot_general(
        left.astype(bf16), right.astype(bf16), (dims, ((), ())), preferred_element_type=f32
    )


def pick_coefficient(step, values):
    result = jnp.float32(values[-1])
    for index in range(len(values) - 1):
        result = jnp.where(step == index, jnp.float32(values[index]), result)
    return result


def kernel(
    n_dom,
    n_sub,
    *refs,
):
    count = 12
    sources, held = refs[:count], refs[-count:]
    (
        out, grad_mat, back_mat, lift_mat, far_mat, cur, early, late, mid, value, coarse,
        zed, dee, faces, slot_rows, near_hot, far_hot, send_buf, recv_buf, send_sem, recv_sem, load_sem,
    ) = refs[count:-count]
    (
        modal, star, normals, speed, jacobian, stiffness,
        lift_minus, lift_plus, cluster, face_source, send_rows, send_counts,
    ) = held
    quants, basis, elems = modal.shape
    rows = cur.shape[0]
    offsets = send_counts.shape[3]
    slots = send_rows.shape[3]
    span = (offsets - 1) // 2
    blocks = offsets * n_sub
    pool_rows = blocks * 2 * slots
    my_dom, my_sub = lax.axis_index("dom"), lax.axis_index("sub")

    def lane(q):
        return slice(q * elems, (q + 1) * elems)

    def partners(step_sign, action):
        for o in range(offsets):
            other = my_dom + step_sign * (o - span)
            for t in range(n_sub):
                good = (other >= 0) & (other < n_dom)
                if o == span:
                    good = my_sub != t

                @pl.when(good)
                def _():
                    action(o, t, other)

    def load(index):
        return pltpu.make_async_copy(sources[index], held[index], load_sem.at[index])

    def wait_for(*wanted):
        for ref in wanted:
            load([ref is other for other in held].index(True)).wait()

    for index in (10, 11, 5, 0, 1, 2, 3, 4, 6, 7, 8, 9):
        load(index).start()
    barrier = pltpu.get_barrier_semaphore()
    recv_buf[...] = jnp.zeros_like(recv_buf)

    def greet(o, t, other):
        pl.semaphore_signal(barrier, inc=1, device_id=(other, t), device_id_type=MESH)

    partners(1, greet)

    wait_for(send_rows, send_counts)
    slot_iota = lax.broadcasted_iota(jnp.int32, (slots, elems), 0)
    for o in range(offsets):
        for t in range(n_sub):
            for part in range(2):
                row = ((o * n_sub + t) * 2 + part) * slots
                ids = jnp.broadcast_to(send_rows[0, part, t, :, o : o + 1], (slots, elems))
                live = jnp.broadcast_to(send_counts[0, part, t : t + 1, o : o + 1], (slots, elems))
                slot_rows[row : row + slots, :] = jnp.where(slot_iota < live, ids, -1)
    send_iota = lax.broadcasted_iota(jnp.int32, (pool_rows, elems), 1)
    send_hot = jnp.where(send_iota == slot_rows[...], 1.0, 0.0)
    slot_list = (lax.broadcasted_iota(jnp.int32, (pool_rows, elems), 0) // slots) % 2

    def place(ref, row, column, matrix):
        high, low = halves(matrix)
        for index, part in enumerate((high, low, high)):
            start = column + index * rows
            ref[row : row + basis, start : start + basis] = part

    grad_mat[...] = jnp.zeros_like(grad_mat)
    wait_for(stiffness)
    for d in range(3):
        place(grad_mat, d * rows, 0, -stiffness[d])
    cur[...] = jnp.zeros_like(cur)
    wait_for(modal)
    for q in range(quants):
        cur[:basis, lane(q)] = modal[q]

    def prepare():
        wait_for(normals, speed, jacobian, lift_minus, lift_plus, cluster, face_source)
        for scratch in (back_mat, lift_mat, far_mat):
            scratch[...] = jnp.zeros_like(scratch)
        for d in range(3):
            place(back_mat, d * rows, 0, stiffness[d].T)
        for f in range(4):
            own, far = 0.5 * lift_minus[:, f, :], 0.5 * lift_plus[:, f, :]
            place(lift_mat.at[f], 0, 0, own)
            place(lift_mat.at[f], 0, 3 * rows, far)
            place(lift_mat.at[f], rows, 0, own)
            place(lift_mat.at[f], rows, 3 * rows, -far)
            place(far_mat.at[f], 0, 0, far)
        coarse_row = cluster[...]
        near_iota = lax.broadcasted_iota(jnp.int32, (elems, elems), 0)
        far_iota = lax.broadcasted_iota(jnp.int32, (pool_rows, elems), 0)
        for f in range(4):
            source = face_source[f : f + 1, :]
            near_hot[:, lane(f)] = jnp.where(near_iota == source, 1.0, 0.0)
            index = source - elems
            block = index // slots
            spot = block * (2 * slots) + (index - block * slots) + slots * coarse_row
            index = jnp.where(index >= 0, spot, -1)
            far_hot[:, lane(f)] = jnp.where(far_iota == index, 1.0, 0.0)

    def stacked(source):
        high, low = halves(source)
        return jnp.concatenate([high, high, low], axis=0).astype(bf16)

    def tall(source):
        return jnp.concatenate([source[:, lane(q)] for q in range(quants)], axis=0)

    def mix(finish):
        group = 3
        for first in range(0, quants, group):
            wanted = range(first, min(first + group, quants))
            total = {q: None for q in wanted}
            for d in range(3):
                for p in range(quants):
                    block = zed[d * rows : (d + 1) * rows, lane(p)]
                    for q in wanted:
                        term = block * star[p, q, d : d + 1, :]
                        total[q] = term if total[q] is None else total[q] + term
            for q in wanted:
                finish(q, total[q])

    def expand(sums):
        def step(index, carry):
            zed[...] = matmul(grad_mat[...], stacked(cur[...]))
            scales = [pick_coefficient(index, values) for _, values in sums]

            def finish(q, total):
                cur[:, lane(q)] = total
                for (ref, _), scale in zip(sums, scales):
                    ref[:, lane(q)] = ref[:, lane(q)] + scale * total

            mix(finish)
            return carry

        lax.fori_loop(0, DEGREE, step, 0)

    def weights(low, high):
        return [
            (high ** (k + 1) - low ** (k + 1)) / float(math.factorial(k + 1))
            for k in range(1, DEGREE + 1)
        ]

    def copy(turn, o, t, other):
        block = o * n_sub + my_sub
        return pltpu.make_async_remote_copy(
            src_ref=send_buf.at[turn, o * n_sub + t],
            dst_ref=recv_buf.at[turn, block],
            send_sem=send_sem.at[turn, o * n_sub + t],
            recv_sem=recv_sem.at[turn, block],
            device_id=(other, t),
            device_id_type=MESH,
        )

    def arrival(turn, o, t, other):
        block = o * n_sub + t
        return pltpu.make_async_remote_copy(
            src_ref=send_buf.at[turn, block],
            dst_ref=recv_buf.at[turn, block],
            send_sem=send_sem.at[turn, block],
            recv_sem=recv_sem.at[turn, block],
            device_id=(other, t),
            device_id_type=MESH,
        )

    def send(turn, picked):
        width = picked.shape[1]
        for block in range(blocks):
            first = block * 2 * slots
            send_buf[turn, block, :, :width] = picked[first : first + 2 * slots, :]
        if turn == 0:
            below = jnp.minimum(my_dom, span)
            above = jnp.minimum(n_dom - 1 - my_dom, span)
            pl.semaphore_wait(barrier, (below + above + 1) * n_sub - 1)
        partners(1, lambda o, t, other: copy(turn, o, t, other).start())

    def pick(hot, source):
        high, low = halves(source)
        return matmul(hot, high, ((1,), (1,))) + matmul(hot, low, ((1,), (1,)))

    wide = quants * rows

    def gathered(left, right):
        high, low = halves(left)
        faces[...] = matmul(jnp.concatenate([high, low], axis=0), right)

    def face_values(f):
        parts = [
            jnp.concatenate(
                [faces[base + q * rows : base + (q + 1) * rows, lane(f)] for q in range(quants)],
                axis=1,
            )
            for base in (0, wide)
        ]
        return jnp.concatenate([parts[0], parts[0], parts[1]], axis=0).astype(bf16)

    def spread(lifted):
        for q in range(quants):
            for d in range(3):
                total = zed[d * rows : (d + 1) * rows, lane(q)]
                for f in range(4):
                    total = total - normals[d, f : f + 1, :] * lifted[f][:rows, lane(q)]
                zed[d * rows : (d + 1) * rows, lane(q)] = total

    def update(turn, integral, near_left, near_right, finish):
        gathered(near_left, near_right)
        own = stacked(integral)
        zed[...] = matmul(back_mat[...], own)
        lifted = [
            matmul(lift_mat[f], jnp.concatenate([own, face_values(f)], axis=0)) for f in range(4)
        ]
        spread(lifted)
        dee[...] = (lifted[0][rows:] + lifted[1][rows:]) + (lifted[2][rows:] + lifted[3][rows:])
        partners(-1, lambda o, t, other: arrival(turn, o, t, other).wait_recv())
        pool = recv_buf[turn].reshape(pool_rows, recv_buf.shape[3])
        gathered(pool.T[:wide], far_hot[...])
        lifted = [matmul(far_mat[f], face_values(f)) for f in range(4)]
        spread(lifted)
        dee[...] -= (lifted[0] + lifted[1]) + (lifted[2] + lifted[3])
        mix(lambda q, total: finish(q, total - speed[...] * dee[:, lane(q)]))

    early[...] = HALF * cur[...]
    late[...] = HALF * cur[...]
    mid[...] = cur[...]
    wait_for(star)
    expand([(early, weights(0.0, HALF)), (late, weights(HALF, 2 * HALF))])
    early_tall = tall(early[...])
    send(0, pick(send_hot, early_tall))
    prepare()
    is_fine = cluster[...] == 0

    def keep_mid(q, total):
        result = mid[:, lane(q)] + jacobian[...] * total
        cur[:, lane(q)] = result
        value[:, lane(q)] = HALF * result
        mid[:, lane(q)] = jnp.where(is_fine, result, mid[:, lane(q)])

    update(0, early[...], early_tall, near_hot[...], keep_mid)
    expand([(value, weights(0.0, HALF))])
    for q in range(quants):
        fine = jnp.where(is_fine, value[:, lane(q)], late[:, lane(q)])
        value[:, lane(q)] = fine
        coarse[:, lane(q)] = early[:, lane(q)] + fine
    both = jnp.concatenate([tall(value[...]), tall(coarse[...])], axis=1)
    both_hot = jnp.concatenate(
        [jnp.where(slot_list == 0, send_hot, 0.0), jnp.where(slot_list == 1, send_hot, 0.0)], axis=1
    )
    send(1, pick(both_hot, both))
    fine_lanes = jnp.concatenate([is_fine.astype(f32)] * 4, axis=1)
    near_both = jnp.concatenate(
        [near_hot[...] * fine_lanes, near_hot[...] * (1.0 - fine_lanes)], axis=0
    )
    for q in range(quants):
        cur[:, lane(q)] = jnp.where(is_fine, value[:, lane(q)], coarse[:, lane(q)])

    def keep_end(q, total):
        out[q] = (mid[:, lane(q)] + jacobian[...] * total)[:basis]

    update(1, cur[...], both, near_both, keep_end)
    for turn in range(2):
        partners(1, lambda o, t, other: copy(turn, o, t, other).wait_send())


def per_device(n_dom, n_sub, modal_state, star_matrices, face_normals, wave_speed, inverse_jacobian,
               stiffness, lift_minus, lift_plus, cluster, face_source, send_rows, send_counts):
    basis, quants, elems = modal_state.shape
    rows = up(basis, 8)
    wide = quants * elems
    blocks = send_counts.shape[2] * n_sub
    slots = send_rows.shape[4]
    pool_rows = blocks * 2 * slots
    message = (2, blocks, 2 * slots, up(quants * rows, 128))
    state = pltpu.VMEM((rows, wide), f32)
    operands = (
        modal_state.transpose(1, 0, 2),
        star_matrices.transpose(1, 2, 0, 3),
        face_normals,
        wave_speed[None],
        inverse_jacobian[None],
        stiffness,
        lift_minus.transpose(1, 0, 2),
        lift_plus.transpose(1, 0, 2),
        cluster[None],
        face_source,
        send_rows.transpose(0, 1, 3, 4, 2),
        send_counts.transpose(0, 1, 3, 2),
    )
    result = pl.pallas_call(
        functools.partial(kernel, n_dom, n_sub),
        out_shape=jax.ShapeDtypeStruct((quants, basis, elems), f32),
        in_specs=[pl.BlockSpec(memory_space=pltpu.HBM)] * len(operands),
        out_specs=pl.BlockSpec(memory_space=pltpu.VMEM),
        scratch_shapes=[
            pltpu.VMEM((3 * rows, 3 * rows), f32),
            pltpu.VMEM((3 * rows, 3 * rows), f32),
            pltpu.VMEM((4, 2 * rows, 6 * rows), f32),
            pltpu.VMEM((4, rows, 3 * rows), f32),
            state,
            state,
            state,
            state,
            state,
            state,
            pltpu.VMEM((3 * rows, wide), f32),
            state,
            pltpu.VMEM((2 * quants * rows, 4 * elems), f32),
            pltpu.VMEM((pool_rows, elems), jnp.int32),
            pltpu.VMEM((elems, 4 * elems), f32),
            pltpu.VMEM((pool_rows, 4 * elems), f32),
            pltpu.VMEM(message, f32),
            pltpu.VMEM(message, f32),
            pltpu.SemaphoreType.DMA((2, blocks)),
            pltpu.SemaphoreType.DMA((2, blocks)),
            pltpu.SemaphoreType.DMA((len(operands),)),
        ]
        + [pltpu.VMEM(operand.shape, operand.dtype) for operand in operands],
        compiler_params=pltpu.CompilerParams(
            collective_id=0, has_side_effects=True, vmem_limit_bytes=60 * 1024 * 1024
        ),
    )(*operands)
    return result.transpose(1, 0, 2)


def solution(mesh):
    placed = (
        P(None, None, ("dom", "sub")),
        P(None, None, None, ("dom", "sub")),
        P(None, None, ("dom", "sub")),
        P(("dom", "sub")),
        P(("dom", "sub")),
        P(),
        P(),
        P(),
        P(("dom", "sub")),
        P(None, ("dom", "sub")),
        P(("dom", "sub"), None, None, None, None),
        P(("dom", "sub"), None, None, None),
    )
    return jax.shard_map(
        functools.partial(per_device, mesh.shape["dom"], mesh.shape["sub"]),
        mesh=mesh,
        in_specs=placed,
        out_specs=P(None, None, ("dom", "sub")),
        check_vma=False,
    )
```

```python
import functools
import math

import jax
import jax.numpy as jnp
from jax import lax
from jax.experimental import pallas as pl
from jax.experimental.pallas import tpu as pltpu
from jax.sharding import PartitionSpec as P

DEGREE = 4
HALF = 0.5
MESH = pl.DeviceIdType.MESH
f32, bf16 = jnp.float32, jnp.bfloat16


def up(value, step):
    return (value + step - 1) // step * step


def halves(value):
    high = value.astype(bf16).astype(f32)
    return high, value - high


def matmul(left, right, dims=((1,), (0,))):
    return lax.dot_general(
        left.astype(bf16), right.astype(bf16), (dims, ((), ())), preferred_element_type=f32
    )


def pick_coefficient(step, values):
    result = jnp.float32(values[-1])
    for index in range(len(values) - 1):
        result = jnp.where(step == index, jnp.float32(values[index]), result)
    return result


def kernel(
    n_dom,
    n_sub,
    *refs,
):
    count = 12
    sources, held = refs[:count], refs[-count:]
    (
        out, grad_mat, back_mat, lift_mat, far_mat, cur, fresh, early, late, mid, value, coarse,
        zed, dee, faces, slot_rows, near_hot, far_hot, send_buf, recv_buf, send_sem, recv_sem, load_sem,
    ) = refs[count:-count]
    (
        modal, star, normals, speed, jacobian, stiffness,
        lift_minus, lift_plus, cluster, face_source, send_rows, send_counts,
    ) = held
    quants, basis, elems = modal.shape
    rows = cur.shape[0]
    offsets = send_counts.shape[3]
    slots = send_rows.shape[3]
    span = (offsets - 1) // 2
    blocks = offsets * n_sub
    pool_rows = blocks * 2 * slots
    my_dom, my_sub = lax.axis_index("dom"), lax.axis_index("sub")

    def lane(q):
        return slice(q * elems, (q + 1) * elems)

    def partners(step_sign, action):
        for o in range(offsets):
            other = my_dom + step_sign * (o - span)
            for t in range(n_sub):
                good = (other >= 0) & (other < n_dom)
                if o == span:
                    good = my_sub != t

                @pl.when(good)
                def _():
                    action(o, t, other)

    def load(index):
        return pltpu.make_async_copy(sources[index], held[index], load_sem.at[index])

    def wait_for(*wanted):
        for ref in wanted:
            load([ref is other for other in held].index(True)).wait()

    for index in (10, 11, 5, 0, 1, 2, 3, 4, 6, 7, 8, 9):
        load(index).start()
    barrier = pltpu.get_barrier_semaphore()
    recv_buf[...] = jnp.zeros_like(recv_buf)

    def greet(o, t, other):
        pl.semaphore_signal(barrier, inc=1, device_id=(other, t), device_id_type=MESH)

    partners(1, greet)

    wait_for(send_rows, send_counts)
    slot_iota = lax.broadcasted_iota(jnp.int32, (slots, elems), 0)
    for o in range(offsets):
        for t in range(n_sub):
            for part in range(2):
                row = ((o * n_sub + t) * 2 + part) * slots
                ids = jnp.broadcast_to(send_rows[0, part, t, :, o : o + 1], (slots, elems))
                live = jnp.broadcast_to(send_counts[0, part, t : t + 1, o : o + 1], (slots, elems))
                slot_rows[row : row + slots, :] = jnp.where(slot_iota < live, ids, -1)
    send_iota = lax.broadcasted_iota(jnp.int32, (pool_rows, elems), 1)
    send_hot = jnp.where(send_iota == slot_rows[...], 1.0, 0.0)
    slot_list = (lax.broadcasted_iota(jnp.int32, (pool_rows, elems), 0) // slots) % 2

    def place(ref, row, column, matrix):
        high, low = halves(matrix)
        for index, part in enumerate((high, low, high)):
            start = column + index * rows
            ref[row : row + basis, start : start + basis] = part

    grad_mat[...] = jnp.zeros_like(grad_mat)
    wait_for(stiffness)
    for d in range(3):
        high, low = halves(-stiffness[d])
        for row, start, part in ((0, 0, high), (0, 3 * rows, high), (rows, 0, low)):
            start += d * rows
            grad_mat[row : row + basis, start : start + basis] = part
    cur[...] = jnp.zeros_like(cur)
    wait_for(modal)
    for q in range(quants):
        cur[:basis, lane(q)] = modal[q]

    def prepare():
        wait_for(normals, speed, jacobian, lift_minus, lift_plus, cluster, face_source)
        for scratch in (back_mat, lift_mat, far_mat):
            scratch[...] = jnp.zeros_like(scratch)
        for d in range(3):
            place(back_mat, d * rows, 0, stiffness[d].T)
        for f in range(4):
            own, far = 0.5 * lift_minus[:, f, :], 0.5 * lift_plus[:, f, :]
            place(lift_mat.at[f], 0, 0, own)
            place(lift_mat.at[f], 0, 3 * rows, far)
            place(lift_mat.at[f], rows, 0, own)
            place(lift_mat.at[f], rows, 3 * rows, -far)
            place(far_mat.at[f], 0, 0, far)
        coarse_row = cluster[...]
        near_iota = lax.broadcasted_iota(jnp.int32, (elems, elems), 0)
        far_iota = lax.broadcasted_iota(jnp.int32, (pool_rows, elems), 0)
        for f in range(4):
            source = face_source[f : f + 1, :]
            near_hot[:, lane(f)] = jnp.where(near_iota == source, 1.0, 0.0)
            index = source - elems
            block = index // slots
            spot = block * (2 * slots) + (index - block * slots) + slots * coarse_row
            index = jnp.where(index >= 0, spot, -1)
            far_hot[:, lane(f)] = jnp.where(far_iota == index, 1.0, 0.0)

    def stacked(source):
        high, low = halves(source)
        return jnp.concatenate([high, high, low], axis=0).astype(bf16)

    def tall(source):
        return jnp.concatenate([source[:, lane(q)] for q in range(quants)], axis=0)

    def mix(finish):
        group = 3
        for first in range(0, quants, group):
            wanted = range(first, min(first + group, quants))
            total = {q: None for q in wanted}
            for d in range(3):
                for p in range(quants):
                    block = zed[d * rows : (d + 1) * rows, lane(p)]
                    for q in wanted:
                        term = block * star[p, q, d : d + 1, :]
                        total[q] = term if total[q] is None else total[q] + term
            for q in wanted:
                finish(q, total[q])

    def expand(sums):
        def step(index, carry):
            scales = [pick_coefficient(index, values) for _, values in sums]
            for first in range(0, quants, 2):
                wanted = range(first, min(first + 2, quants))
                mixed = []
                for q in wanted:
                    totals = [None] * 3
                    for p in range(quants):
                        block = cur[:, lane(p)]
                        for d in range(3):
                            term = block * star[p, q, d : d + 1, :]
                            totals[d] = term if totals[d] is None else totals[d] + term
                    high, low = halves(jnp.concatenate(totals, axis=0))
                    mixed.append(jnp.concatenate([high, low], axis=0).astype(bf16))
                product = matmul(grad_mat[...], jnp.concatenate(mixed, axis=1))
                product = product[:rows] + product[rows:]
                for q in wanted:
                    total = product[:, lane(q - first)]
                    fresh[:, lane(q)] = total
                    for (ref, _), scale in zip(sums, scales):
                        ref[:, lane(q)] = ref[:, lane(q)] + scale * total
            cur[...] = fresh[...]
            return carry

        lax.fori_loop(0, DEGREE, step, 0)

    def weights(low, high):
        return [
            (high ** (k + 1) - low ** (k + 1)) / float(math.factorial(k + 1))
            for k in range(1, DEGREE + 1)
        ]

    def copy(turn, o, t, other):
        block = o * n_sub + my_sub
        return pltpu.make_async_remote_copy(
            src_ref=send_buf.at[turn, o * n_sub + t],
            dst_ref=recv_buf.at[turn, block],
            send_sem=send_sem.at[turn, o * n_sub + t],
            recv_sem=recv_sem.at[turn, block],
            device_id=(other, t),
            device_id_type=MESH,
        )

    def arrival(turn, o, t, other):
        block = o * n_sub + t
        return pltpu.make_async_remote_copy(
            src_ref=send_buf.at[turn, block],
            dst_ref=recv_buf.at[turn, block],
            send_sem=send_sem.at[turn, block],
            recv_sem=recv_sem.at[turn, block],
            device_id=(other, t),
            device_id_type=MESH,
        )

    def send(turn, picked):
        width = picked.shape[1]
        for block in range(blocks):
            first = block * 2 * slots
            send_buf[turn, block, :, :width] = picked[first : first + 2 * slots, :]
        if turn == 0:
            below = jnp.minimum(my_dom, span)
            above = jnp.minimum(n_dom - 1 - my_dom, span)
            pl.semaphore_wait(barrier, (below + above + 1) * n_sub - 1)
        partners(1, lambda o, t, other: copy(turn, o, t, other).start())

    def pick(hot, source):
        high, low = halves(source)
        return matmul(hot, high, ((1,), (1,))) + matmul(hot, low, ((1,), (1,)))

    wide = quants * rows

    def gathered(left, right):
        high, low = halves(left)
        faces[...] = matmul(jnp.concatenate([high, low], axis=0), right)

    def face_values(f):
        parts = [
            jnp.concatenate(
                [faces[base + q * rows : base + (q + 1) * rows, lane(f)] for q in range(quants)],
                axis=1,
            )
            for base in (0, wide)
        ]
        return jnp.concatenate([parts[0], parts[0], parts[1]], axis=0).astype(bf16)

    def spread(lifted):
        for q in range(quants):
            for d in range(3):
                total = zed[d * rows : (d + 1) * rows, lane(q)]
                for f in range(4):
                    total = total - normals[d, f : f + 1, :] * lifted[f][:rows, lane(q)]
                zed[d * rows : (d + 1) * rows, lane(q)] = total

    def update(turn, integral, near_left, near_right, finish):
        gathered(near_left, near_right)
        own = stacked(integral)
        zed[...] = matmul(back_mat[...], own)
        lifted = [
            matmul(lift_mat[f], jnp.concatenate([own, face_values(f)], axis=0)) for f in range(4)
        ]
        spread(lifted)
        dee[...] = (lifted[0][rows:] + lifted[1][rows:]) + (lifted[2][rows:] + lifted[3][rows:])
        partners(-1, lambda o, t, other: arrival(turn, o, t, other).wait_recv())
        pool = recv_buf[turn].reshape(pool_rows, recv_buf.shape[3])
        gathered(pool.T[:wide], far_hot[...])
        lifted = [matmul(far_mat[f], face_values(f)) for f in range(4)]
        spread(lifted)
        dee[...] -= (lifted[0] + lifted[1]) + (lifted[2] + lifted[3])
        mix(lambda q, total: finish(q, total - speed[...] * dee[:, lane(q)]))

    early[...] = HALF * cur[...]
    late[...] = HALF * cur[...]
    mid[...] = cur[...]
    wait_for(star)
    expand([(early, weights(0.0, HALF)), (late, weights(HALF, 2 * HALF))])
    early_tall = tall(early[...])
    send(0, pick(send_hot, early_tall))
    prepare()
    is_fine = cluster[...] == 0

    def keep_mid(q, total):
        change = jacobian[...] * total
        result = mid[:, lane(q)] + change
        cur[:, lane(q)] = result
        value[:, lane(q)] = HALF * result
        mid[:, lane(q)] = jnp.where(is_fine, change, 0.0)

    update(0, early[...], early_tall, near_hot[...], keep_mid)
    expand([(value, weights(0.0, HALF))])
    for q in range(quants):
        fine = jnp.where(is_fine, value[:, lane(q)], late[:, lane(q)])
        value[:, lane(q)] = fine
        coarse[:, lane(q)] = early[:, lane(q)] + fine
    both = jnp.concatenate([tall(value[...]), tall(coarse[...])], axis=1)
    both_hot = jnp.concatenate(
        [jnp.where(slot_list == 0, send_hot, 0.0), jnp.where(slot_list == 1, send_hot, 0.0)], axis=1
    )
    send(1, pick(both_hot, both))
    fine_lanes = jnp.concatenate([is_fine.astype(f32)] * 4, axis=1)
    near_both = jnp.concatenate(
        [near_hot[...] * fine_lanes, near_hot[...] * (1.0 - fine_lanes)], axis=0
    )
    for q in range(quants):
        cur[:, lane(q)] = jnp.where(is_fine, value[:, lane(q)], coarse[:, lane(q)])

    def keep_end(q, total):
        out[q] = (mid[:, lane(q)] + jacobian[...] * total)[:basis]

    update(1, cur[...], both, near_both, keep_end)
    for turn in range(2):
        partners(1, lambda o, t, other: copy(turn, o, t, other).wait_send())


def per_device(n_dom, n_sub, modal_state, star_matrices, face_normals, wave_speed, inverse_jacobian,
               stiffness, lift_minus, lift_plus, cluster, face_source, send_rows, send_counts):
    basis, quants, elems = modal_state.shape
    rows = up(basis, 8)
    wide = quants * elems
    blocks = send_counts.shape[2] * n_sub
    slots = send_rows.shape[4]
    pool_rows = blocks * 2 * slots
    message = (2, blocks, 2 * slots, up(quants * rows, 128))
    state = pltpu.VMEM((rows, wide), f32)
    operands = (
        modal_state.transpose(1, 0, 2),
        star_matrices.transpose(1, 2, 0, 3),
        face_normals,
        wave_speed[None],
        inverse_jacobian[None],
        stiffness,
        lift_minus.transpose(1, 0, 2),
        lift_plus.transpose(1, 0, 2),
        cluster[None],
        face_source,
        send_rows.transpose(0, 1, 3, 4, 2),
        send_counts.transpose(0, 1, 3, 2),
    )
    result = pl.pallas_call(
        functools.partial(kernel, n_dom, n_sub),
        out_shape=jax.ShapeDtypeStruct((quants, basis, elems), f32),
        in_specs=[pl.BlockSpec(memory_space=pltpu.HBM)] * len(operands),
        out_specs=pl.BlockSpec(memory_space=pltpu.VMEM),
        scratch_shapes=[
            pltpu.VMEM((2 * rows, 6 * rows), f32),
            pltpu.VMEM((3 * rows, 3 * rows), f32),
            pltpu.VMEM((4, 2 * rows, 6 * rows), f32),
            pltpu.VMEM((4, rows, 3 * rows), f32),
            state,
            state,
            state,
            state,
            state,
            state,
            state,
            pltpu.VMEM((3 * rows, wide), f32),
            state,
            pltpu.VMEM((2 * quants * rows, 4 * elems), f32),
            pltpu.VMEM((pool_rows, elems), jnp.int32),
            pltpu.VMEM((elems, 4 * elems), f32),
            pltpu.VMEM((pool_rows, 4 * elems), f32),
            pltpu.VMEM(message, f32),
            pltpu.VMEM(message, f32),
            pltpu.SemaphoreType.DMA((2, blocks)),
            pltpu.SemaphoreType.DMA((2, blocks)),
            pltpu.SemaphoreType.DMA((len(operands),)),
        ]
        + [pltpu.VMEM(operand.shape, operand.dtype) for operand in operands],
        compiler_params=pltpu.CompilerParams(
            collective_id=0, has_side_effects=True, vmem_limit_bytes=60 * 1024 * 1024
        ),
    )(*operands)
    return modal_state + result.transpose(1, 0, 2)


def solution(mesh):
    placed = (
        P(None, None, ("dom", "sub")),
        P(None, None, None, ("dom", "sub")),
        P(None, None, ("dom", "sub")),
        P(("dom", "sub")),
        P(("dom", "sub")),
        P(),
        P(),
        P(),
        P(("dom", "sub")),
        P(None, ("dom", "sub")),
        P(("dom", "sub"), None, None, None, None),
        P(("dom", "sub"), None, None, None),
    )
    return jax.shard_map(
        functools.partial(per_device, mesh.shape["dom"], mesh.shape["sub"]),
        mesh=mesh,
        in_specs=placed,
        out_specs=P(None, None, ("dom", "sub")),
        check_vma=False,
    )
```

```python
import functools
import math

import jax
import jax.numpy as jnp
from jax import lax
from jax.experimental import pallas as pl
from jax.experimental.pallas import tpu as pltpu
from jax.sharding import PartitionSpec as P

DEGREE = 4
HALF = 0.5
MESH = pl.DeviceIdType.MESH
f32, bf16 = jnp.float32, jnp.bfloat16


def up(value, step):
    return (value + step - 1) // step * step


def halves(value):
    high = value.astype(bf16).astype(f32)
    return high, value - high


def matmul(left, right, dims=((1,), (0,))):
    return lax.dot_general(
        left.astype(bf16), right.astype(bf16), (dims, ((), ())), preferred_element_type=f32
    )


def pick_coefficient(step, values):
    result = jnp.float32(values[-1])
    for index in range(len(values) - 1):
        result = jnp.where(step == index, jnp.float32(values[index]), result)
    return result


def kernel(
    n_dom,
    n_sub,
    *refs,
):
    count = 12
    sources, held = refs[:count], refs[-count:]
    (
        out, grad_mat, back_mat, lift_mat, far_mat, cur, fresh, early, late, mid, value, coarse,
        zed, dee, faces, slot_rows, near_hot, far_hot, send_buf, recv_buf, send_sem, recv_sem, load_sem,
    ) = refs[count:-count]
    (
        modal, star, normals, speed, jacobian, stiffness,
        lift_minus, lift_plus, cluster, face_source, send_rows, send_counts,
    ) = held
    quants, basis, elems = modal.shape
    rows = cur.shape[0]
    offsets = send_counts.shape[3]
    slots = send_rows.shape[3]
    span = (offsets - 1) // 2
    blocks = offsets * n_sub
    pool_rows = blocks * 2 * slots
    my_dom, my_sub = lax.axis_index("dom"), lax.axis_index("sub")

    def lane(q):
        return slice(q * elems, (q + 1) * elems)

    def partners(step_sign, action):
        for o in range(offsets):
            other = my_dom + step_sign * (o - span)
            for t in range(n_sub):
                good = (other >= 0) & (other < n_dom)
                if o == span:
                    good = my_sub != t

                @pl.when(good)
                def _():
                    action(o, t, other)

    def load(index):
        return pltpu.make_async_copy(sources[index], held[index], load_sem.at[index])

    def wait_for(*wanted):
        for ref in wanted:
            load([ref is other for other in held].index(True)).wait()

    for index in (10, 11, 5, 0, 1, 2, 3, 4, 6, 7, 8, 9):
        load(index).start()
    barrier = pltpu.get_barrier_semaphore()
    recv_buf[...] = jnp.zeros_like(recv_buf)

    def greet(o, t, other):
        pl.semaphore_signal(barrier, inc=1, device_id=(other, t), device_id_type=MESH)

    partners(1, greet)

    wait_for(send_rows, send_counts)
    slot_iota = lax.broadcasted_iota(jnp.int32, (slots, elems), 0)
    for o in range(offsets):
        for t in range(n_sub):
            for part in range(2):
                row = ((o * n_sub + t) * 2 + part) * slots
                ids = jnp.broadcast_to(send_rows[0, part, t, :, o : o + 1], (slots, elems))
                live = jnp.broadcast_to(send_counts[0, part, t : t + 1, o : o + 1], (slots, elems))
                slot_rows[row : row + slots, :] = jnp.where(slot_iota < live, ids, -1)
    send_iota = lax.broadcasted_iota(jnp.int32, (pool_rows, elems), 1)
    send_hot = jnp.where(send_iota == slot_rows[...], 1.0, 0.0)
    slot_list = (lax.broadcasted_iota(jnp.int32, (pool_rows, elems), 0) // slots) % 2

    def place(ref, row, column, matrix):
        high, low = halves(matrix)
        for index, part in enumerate((high, low, high)):
            start = column + index * rows
            ref[row : row + basis, start : start + basis] = part

    grad_mat[...] = jnp.zeros_like(grad_mat)
    wait_for(stiffness)
    for d in range(3):
        high, low = halves(-stiffness[d])
        for row, start, part in ((0, 0, high), (0, 3 * rows, high), (rows, 0, low)):
            start += d * rows
            grad_mat[row : row + basis, start : start + basis] = part
    cur[...] = jnp.zeros_like(cur)
    wait_for(modal)
    for q in range(quants):
        cur[:basis, lane(q)] = modal[q]

    def prepare():
        wait_for(normals, speed, jacobian, lift_minus, lift_plus, cluster, face_source)
        for scratch in (back_mat, lift_mat, far_mat):
            scratch[...] = jnp.zeros_like(scratch)
        for d in range(3):
            place(back_mat, d * rows, 0, stiffness[d].T)
        for f in range(4):
            own, far = 0.5 * lift_minus[:, f, :], 0.5 * lift_plus[:, f, :]
            place(lift_mat.at[f], 0, 0, own)
            place(lift_mat.at[f], 0, 3 * rows, far)
            place(lift_mat.at[f], rows, 0, own)
            place(lift_mat.at[f], rows, 3 * rows, -far)
            place(far_mat.at[f], 0, 0, far)
        coarse_row = cluster[...]
        near_iota = lax.broadcasted_iota(jnp.int32, (elems, elems), 0)
        far_iota = lax.broadcasted_iota(jnp.int32, (pool_rows, elems), 0)
        for f in range(4):
            source = face_source[f : f + 1, :]
            near_hot[:, lane(f)] = jnp.where(near_iota == source, 1.0, 0.0)
            index = source - elems
            block = index // slots
            spot = block * (2 * slots) + (index - block * slots) + slots * coarse_row
            index = jnp.where(index >= 0, spot, -1)
            far_hot[:, lane(f)] = jnp.where(far_iota == index, 1.0, 0.0)

    def stacked(source):
        high, low = halves(source)
        return jnp.concatenate([high, high, low], axis=0).astype(bf16)

    def tall(source):
        return jnp.concatenate([source[:, lane(q)] for q in range(quants)], axis=0)

    def mix(finish):
        group = 3
        for first in range(0, quants, group):
            wanted = range(first, min(first + group, quants))
            total = {q: None for q in wanted}
            for d in range(3):
                for p in range(quants):
                    block = zed[d * rows : (d + 1) * rows, lane(p)]
                    for q in wanted:
                        term = block * star[p, q, d : d + 1, :]
                        total[q] = term if total[q] is None else total[q] + term
            for q in wanted:
                finish(q, total[q])

    def expand(sums):
        def step(index, carry):
            scales = [pick_coefficient(index, values) for _, values in sums]
            for first in range(0, quants, 2):
                wanted = range(first, min(first + 2, quants))
                mixed = []
                for q in wanted:
                    totals = [None] * 3
                    for p in range(quants):
                        block = cur[:, lane(p)]
                        for d in range(3):
                            term = block * star[p, q, d : d + 1, :]
                            totals[d] = term if totals[d] is None else totals[d] + term
                    high, low = halves(jnp.concatenate(totals, axis=0))
                    mixed.append(jnp.concatenate([high, low], axis=0).astype(bf16))
                product = matmul(grad_mat[...], jnp.concatenate(mixed, axis=1))
                product = product[:rows] + product[rows:]
                for q in wanted:
                    total = product[:, lane(q - first)]
                    fresh[:, lane(q)] = total
                    for (ref, _), scale in zip(sums, scales):
                        ref[:, lane(q)] = ref[:, lane(q)] + scale * total
            cur[...] = fresh[...]
            return carry

        lax.fori_loop(0, DEGREE, step, 0)

    def weights(low, high):
        return [
            (high ** (k + 1) - low ** (k + 1)) / float(math.factorial(k + 1))
            for k in range(1, DEGREE + 1)
        ]

    def copy(turn, o, t, other):
        block = o * n_sub + my_sub
        return pltpu.make_async_remote_copy(
            src_ref=send_buf.at[turn, o * n_sub + t],
            dst_ref=recv_buf.at[turn, block],
            send_sem=send_sem.at[turn, o * n_sub + t],
            recv_sem=recv_sem.at[turn, block],
            device_id=(other, t),
            device_id_type=MESH,
        )

    def arrival(turn, o, t, other):
        block = o * n_sub + t
        return pltpu.make_async_remote_copy(
            src_ref=send_buf.at[turn, block],
            dst_ref=recv_buf.at[turn, block],
            send_sem=send_sem.at[turn, block],
            recv_sem=recv_sem.at[turn, block],
            device_id=(other, t),
            device_id_type=MESH,
        )

    def send(turn, picked):
        width = picked.shape[1]
        for block in range(blocks):
            first = block * 2 * slots
            send_buf[turn, block, :, :width] = picked[first : first + 2 * slots, :]
        if turn == 0:
            below = jnp.minimum(my_dom, span)
            above = jnp.minimum(n_dom - 1 - my_dom, span)
            pl.semaphore_wait(barrier, (below + above + 1) * n_sub - 1)
        partners(1, lambda o, t, other: copy(turn, o, t, other).start())

    def pick(hot, source):
        high, low = halves(source)
        return matmul(hot, high, ((1,), (1,))) + matmul(hot, low, ((1,), (1,)))

    wide = quants * rows

    def gathered(left, right):
        high, low = halves(left)
        faces[...] = matmul(jnp.concatenate([high, low], axis=0), right)

    def face_values(f):
        parts = [
            jnp.concatenate(
                [faces[base + q * rows : base + (q + 1) * rows, lane(f)] for q in range(quants)],
                axis=1,
            )
            for base in (0, wide)
        ]
        return jnp.concatenate([parts[0], parts[0], parts[1]], axis=0).astype(bf16)

    def spread(lifted):
        for q in range(quants):
            for d in range(3):
                total = zed[d * rows : (d + 1) * rows, lane(q)]
                for f in range(4):
                    total = total - normals[d, f : f + 1, :] * lifted[f][:rows, lane(q)]
                zed[d * rows : (d + 1) * rows, lane(q)] = total

    def update(turn, integral, near_left, near_right, finish):
        gathered(near_left, near_right)
        own = stacked(integral)
        zed[...] = matmul(back_mat[...], own)
        lifted = [
            matmul(lift_mat[f], jnp.concatenate([own, face_values(f)], axis=0)) for f in range(4)
        ]
        spread(lifted)
        dee[...] = (lifted[0][rows:] + lifted[1][rows:]) + (lifted[2][rows:] + lifted[3][rows:])
        partners(-1, lambda o, t, other: arrival(turn, o, t, other).wait_recv())
        pool = recv_buf[turn].reshape(pool_rows, recv_buf.shape[3])
        gathered(pool.T[:wide], far_hot[...])
        lifted = [matmul(far_mat[f], face_values(f)) for f in range(4)]
        spread(lifted)
        dee[...] -= (lifted[0] + lifted[1]) + (lifted[2] + lifted[3])
        mix(lambda q, total: finish(q, total - speed[...] * dee[:, lane(q)]))

    early[...] = HALF * cur[...]
    late[...] = HALF * cur[...]
    mid[...] = cur[...]
    wait_for(star)
    expand([(early, weights(0.0, HALF)), (late, weights(HALF, 2 * HALF))])
    early_tall = tall(early[...])
    send(0, pick(send_hot, early_tall))
    prepare()
    is_fine = cluster[...] == 0

    def keep_mid(q, total):
        change = jacobian[...] * total
        result = mid[:, lane(q)] + change
        cur[:, lane(q)] = result
        value[:, lane(q)] = HALF * result
        mid[:, lane(q)] = jnp.where(is_fine, change, 0.0)

    update(0, early[...], early_tall, near_hot[...], keep_mid)
    expand([(value, weights(0.0, HALF))])
    for q in range(quants):
        fine = jnp.where(is_fine, value[:, lane(q)], late[:, lane(q)])
        value[:, lane(q)] = fine
        coarse[:, lane(q)] = early[:, lane(q)] + fine
    both = jnp.concatenate([tall(value[...]), tall(coarse[...])], axis=1)
    both_hot = jnp.concatenate(
        [jnp.where(slot_list == 0, send_hot, 0.0), jnp.where(slot_list == 1, send_hot, 0.0)], axis=1
    )
    send(1, pick(both_hot, both))
    fine_lanes = jnp.concatenate([is_fine.astype(f32)] * 4, axis=1)
    near_both = jnp.concatenate(
        [near_hot[...] * fine_lanes, near_hot[...] * (1.0 - fine_lanes)], axis=0
    )
    for q in range(quants):
        cur[:, lane(q)] = jnp.where(is_fine, value[:, lane(q)], coarse[:, lane(q)])

    def keep_end(q, total):
        out[q] = modal[q] + (mid[:, lane(q)] + jacobian[...] * total)[:basis]

    update(1, cur[...], both, near_both, keep_end)
    for turn in range(2):
        partners(1, lambda o, t, other: copy(turn, o, t, other).wait_send())


def per_device(n_dom, n_sub, modal_state, star_matrices, face_normals, wave_speed, inverse_jacobian,
               stiffness, lift_minus, lift_plus, cluster, face_source, send_rows, send_counts):
    basis, quants, elems = modal_state.shape
    rows = up(basis, 8)
    wide = quants * elems
    blocks = send_counts.shape[2] * n_sub
    slots = send_rows.shape[4]
    pool_rows = blocks * 2 * slots
    message = (2, blocks, 2 * slots, up(quants * rows, 128))
    state = pltpu.VMEM((rows, wide), f32)
    operands = (
        modal_state.transpose(1, 0, 2),
        star_matrices.transpose(1, 2, 0, 3),
        face_normals,
        wave_speed[None],
        inverse_jacobian[None],
        stiffness,
        lift_minus.transpose(1, 0, 2),
        lift_plus.transpose(1, 0, 2),
        cluster[None],
        face_source,
        send_rows.transpose(0, 1, 3, 4, 2),
        send_counts.transpose(0, 1, 3, 2),
    )
    result = pl.pallas_call(
        functools.partial(kernel, n_dom, n_sub),
        out_shape=pltpu.VMEM((quants, basis, elems), f32),
        in_specs=[pl.BlockSpec(memory_space=pltpu.HBM)] * len(operands),
        out_specs=pl.BlockSpec(memory_space=pltpu.VMEM),
        scratch_shapes=[
            pltpu.VMEM((2 * rows, 6 * rows), f32),
            pltpu.VMEM((3 * rows, 3 * rows), f32),
            pltpu.VMEM((4, 2 * rows, 6 * rows), f32),
            pltpu.VMEM((4, rows, 3 * rows), f32),
            state,
            state,
            state,
            state,
            state,
            state,
            state,
            pltpu.VMEM((3 * rows, wide), f32),
            state,
            pltpu.VMEM((2 * quants * rows, 4 * elems), f32),
            pltpu.VMEM((pool_rows, elems), jnp.int32),
            pltpu.VMEM((elems, 4 * elems), f32),
            pltpu.VMEM((pool_rows, 4 * elems), f32),
            pltpu.VMEM(message, f32),
            pltpu.VMEM(message, f32),
            pltpu.SemaphoreType.DMA((2, blocks)),
            pltpu.SemaphoreType.DMA((2, blocks)),
            pltpu.SemaphoreType.DMA((len(operands),)),
        ]
        + [pltpu.VMEM(operand.shape, operand.dtype) for operand in operands],
        compiler_params=pltpu.CompilerParams(
            collective_id=0, has_side_effects=True, vmem_limit_bytes=60 * 1024 * 1024
        ),
    )(*operands)
    return result.transpose(1, 0, 2)


def solution(mesh):
    placed = (
        P(None, None, ("dom", "sub")),
        P(None, None, None, ("dom", "sub")),
        P(None, None, ("dom", "sub")),
        P(("dom", "sub")),
        P(("dom", "sub")),
        P(),
        P(),
        P(),
        P(("dom", "sub")),
        P(None, ("dom", "sub")),
        P(("dom", "sub"), None, None, None, None),
        P(("dom", "sub"), None, None, None),
    )
    return jax.shard_map(
        functools.partial(per_device, mesh.shape["dom"], mesh.shape["sub"]),
        mesh=mesh,
        in_specs=placed,
        out_specs=P(None, None, ("dom", "sub")),
        check_vma=False,
    )
```
